128 devices in a mesh: ctx: 16 (over z, y), tp: 8 (over x, core).
Axes of the slice: x: 4, y: 4, z: 4, core: 2. Of those that a mesh axis runs over, the one named last changes fastest.
Arguments:
- signal: bfloat16 [8192, 4096], P('ctx', 'tp'), may hold values from -6 to 6
- gate: bfloat16 [8192, 4096], P('ctx', 'tp'), may hold values from -6 to 6
- filt: float32 [8192, 4096], P('ctx', 'tp'), may hold values from -0.0625 to 0.0625
- skip: float32 [4096], P('tp'), may hold values from 0.5 to 1.5
- w_out: bfloat16 [4096, 8192], P(None, 'tp'), may hold values from -0.09375 to 0.09375
Outputs:
- output: bfloat16 [8192, 8192], P('ctx', 'tp')
The draws below stay inside these ranges and needn't reach their ends.
All inputs are finite; a program needn't handle non-finite values.
Results may differ from the reference program's by a relative error of at most 0.015.
Values may be sent and summed in bfloat16 or wider, within the bound.
No kernel may reach another device: no remote copies, remote signals or barrier semaphores. Data moves between devices by JAX's collectives and lax.ppermute only.
A program may use at most 128 MiB of HBM per device.

```python
import jax
import jax.numpy as jnp

D = 8192
C = 4096
SEQ = 8192


def shard_levels(stream_key, extent, cuts, least, largest):
    def one(dim, parts):
        heights = jax.random.uniform(jax.random.fold_in(jax.random.fold_in(stream_key, 6), dim), (parts,), jnp.float32, least / len(cuts), largest / len(cuts))
        return jnp.repeat(jnp.exp(heights), extent[dim] // parts).reshape((-1,) + (1,) * (len(extent) - dim - 1))

    factor_of = one(*cuts[0])
    for cut in cuts[1:]:
        factor_of = factor_of * one(*cut)
    return factor_of


def scatter_about(own_key, dims, spread, bound, shards=(), held_as=jnp.bfloat16):
    entries = spread * jax.random.normal(own_key, dims, jnp.float32)
    if shards:
        entries = entries * shard_levels(own_key, dims, shards, -0.22, 0.18)
    return jnp.clip(entries, -bound, bound).astype(held_as)


def setup_inputs(seed: int = 0) -> dict:
    key_of = jax.random.split(jax.random.key(seed), 6)
    return {
        "signal": scatter_about(key_of[0], (SEQ, C), 1.0, 6.0, ((0, 16), (1, 8))),
        "gate": scatter_about(key_of[1], (SEQ, C), 1.0, 6.0, ((0, 16), (1, 8))),
        "filt": scatter_about(key_of[2], (SEQ, C), SEQ ** -0.5, 0.0625, ((0, 16), (1, 8)), jnp.float32),
        "skip": jnp.clip(0.5 + 1.0 * jax.random.uniform(key_of[3], (C,), jnp.float32) ** shard_levels(key_of[3], (C,), ((0, 8),), -0.2, 0.2), 0.5, 1.5),
        "w_out": scatter_about(key_of[4], (C, D), C ** -0.5, 0.09375, ((1, 8),)),
    }


def reference(signal, gate, filt, skip, w_out):
    padded_len = 2 * SEQ
    values = signal.astype(jnp.float32)
    spectrum = jnp.fft.rfft(values, n=padded_len, axis=0) * jnp.fft.rfft(filt, n=padded_len, axis=0)
    convolved = jnp.fft.irfft(spectrum, n=padded_len, axis=0)[:SEQ]
    mixed = (gate.astype(jnp.float32) * (convolved + skip * values)).astype(jnp.bfloat16)
    return jnp.dot(mixed, w_out, preferred_element_type=jnp.float32).astype(jnp.bfloat16)
```

```python
import jax
import jax.numpy as jnp
import numpy as np
from jax import lax
from jax.experimental import pallas as pl
from jax.experimental.pallas import tpu as pltpu
from jax.sharding import PartitionSpec as P

GROUP = 16


def tables(blocks, rows):
    length = blocks * rows
    freq = np.arange(blocks) + 0.25
    turn = 2 * np.pi * np.outer(freq, np.arange(blocks)) / blocks
    same = np.eye(GROUP)
    first = np.concatenate([np.kron(np.cos(turn), same), np.kron(-np.sin(turn), same)], axis=0)
    last = np.concatenate([np.kron(np.cos(turn.T), same), np.kron(-np.sin(turn.T), same)], axis=1)
    twist = np.repeat(2 * np.pi * np.outer(freq, np.arange(rows)) / length, GROUP, axis=0)
    index = np.arange(rows)
    inner = 2 * np.pi * (np.outer(index, index) % rows) / rows
    cos, sin = np.cos(inner), np.sin(inner)
    middle = np.block([[cos, -sin], [sin, cos]])
    return (
        first.astype(jnp.bfloat16),
        middle.astype(jnp.bfloat16),
        (last / length).astype(jnp.bfloat16),
        np.cos(twist).astype(np.float32),
        np.sin(twist).astype(np.float32),
    )


def dot(left, right):
    return jnp.dot(left, right, preferred_element_type=jnp.float32)


def turn_kernel(signal_ref, filt_ref, out_ref):
    share = out_ref.shape[1] // 2
    for part, ref in enumerate((signal_ref, filt_ref)):
        flipped = ref[...].astype(jnp.float32).T.astype(jnp.bfloat16)
        out_ref[:, part * share : (part + 1) * share, :] = flipped.reshape(-1, share, flipped.shape[1])


def turn(signal, filt, ways):
    rows, channels = signal.shape
    share = channels // ways
    lanes = 128
    return pl.pallas_call(
        turn_kernel,
        grid=(channels // lanes,),
        in_specs=[pl.BlockSpec((rows, lanes), lambda b: (0, b))] * 2,
        out_specs=pl.BlockSpec((lanes // share, 2 * share, rows), lambda b: (b, 0, 0)),
        out_shape=jax.ShapeDtypeStruct((ways, 2 * share, rows), jnp.bfloat16),
        name="turn",
    )(signal, filt)


def conv_kernel(x_ref, first_ref, middle_ref, last_ref, cos_ref, sin_ref, out_ref):
    blocks, doubled, rows = x_ref.shape
    share = doubled // 2
    half = blocks * GROUP
    cos, sin = cos_ref[...], sin_ref[...]
    for start in range(0, share, GROUP):
        parts = []
        for base in (start, share + start):
            x = x_ref[:, base : base + GROUP, :].reshape(half, rows)
            a = dot(first_ref[...], x)
            re, im = a[:half], a[half:]
            parts.append(
                jnp.concatenate([re * cos + im * sin, im * cos - re * sin], axis=1).astype(jnp.bfloat16)
            )
        spec = dot(jnp.concatenate(parts, axis=0), middle_ref[...])
        xr, xi = spec[:half, :rows], spec[:half, rows:]
        hr, hi = spec[half:, :rows], spec[half:, rows:]
        prod = jnp.concatenate([xr * hr - xi * hi, xr * hi + xi * hr], axis=1).astype(jnp.bfloat16)
        back = lax.dot_general(
            prod, middle_ref[...], (((1,), (1,)), ((), ())), preferred_element_type=jnp.float32
        )
        re, im = back[:, :rows], back[:, rows:]
        untwisted = jnp.concatenate([re * cos - im * sin, re * sin + im * cos], axis=0).astype(jnp.bfloat16)
        y = dot(last_ref[...], untwisted)
        out_ref[:, start : start + GROUP, :] = y.reshape(blocks, GROUP, rows).astype(jnp.bfloat16)


def convolve(x):
    blocks, doubled, rows = x.shape
    constants = [jnp.asarray(t) for t in tables(blocks, rows)]
    return pl.pallas_call(
        conv_kernel,
        out_shape=jax.ShapeDtypeStruct((blocks, doubled // 2, rows), jnp.bfloat16),
        compiler_params=pltpu.CompilerParams(vmem_limit_bytes=48 * 2**20),
        name="convolve",
    )(x, *constants)


def mix_kernel(conv_ref, signal_ref, gate_ref, skip_ref, out_ref):
    conv = conv_ref[...].astype(jnp.float32).T
    values = signal_ref[...].astype(jnp.float32)
    out_ref[...] = (gate_ref[...].astype(jnp.float32) * (conv + skip_ref[...] * values)).astype(jnp.bfloat16)


def mix(conv, signal, gate, skip):
    rows, channels = signal.shape
    lanes = 128
    wide = pl.BlockSpec((rows, lanes), lambda b: (0, b))
    return pl.pallas_call(
        mix_kernel,
        grid=(channels // lanes,),
        in_specs=[
            pl.BlockSpec((lanes, rows), lambda b: (b, 0)),
            wide,
            wide,
            pl.BlockSpec((1, lanes), lambda b: (0, b)),
        ],
        out_specs=wide,
        out_shape=jax.ShapeDtypeStruct((rows, channels), jnp.bfloat16),
        name="mix",
    )(conv, signal, gate, skip.reshape(1, channels))


def per_device(signal, gate, filt, skip, w_out):
    ways = lax.axis_size("ctx")
    rows, channels = signal.shape
    spread = lax.all_to_all(turn(signal, filt, ways), "ctx", 0, 0, tiled=True)
    conv = lax.all_to_all(convolve(spread), "ctx", 0, 0, tiled=True)
    mixed = mix(conv.reshape(channels, rows), signal, gate, skip)
    result = jnp.dot(
        lax.all_gather(mixed, "tp", axis=1, tiled=True), w_out, preferred_element_type=jnp.float32
    )
    return result.astype(jnp.bfloat16)


def solution(mesh):
    return jax.shard_map(
        per_device,
        mesh=mesh,
        in_specs=(P("ctx", "tp"), P("ctx", "tp"), P("ctx", "tp"), P("tp"), P(None, "tp")),
        out_specs=P("ctx", "tp"),
        check_vma=False,
    )
```

```python
import functools

import jax
import jax.numpy as jnp
import numpy as np
from jax import lax
from jax.experimental import pallas as pl
from jax.experimental.pallas import tpu as pltpu
from jax.sharding import PartitionSpec as P

GROUP = 16


def tables(blocks, rows):
    length = blocks * rows
    freq = np.arange(blocks) + 0.25
    turn = 2 * np.pi * np.outer(freq, np.arange(blocks)) / blocks
    same = np.eye(GROUP)
    first = np.concatenate([np.kron(np.cos(turn), same), np.kron(-np.sin(turn), same)], axis=0)
    last = np.concatenate([np.kron(np.cos(turn.T), same), np.kron(-np.sin(turn.T), same)], axis=1)
    twist = np.repeat(2 * np.pi * np.outer(freq, np.arange(rows)) / length, GROUP, axis=0)
    index = np.arange(rows)
    inner = 2 * np.pi * (np.outer(index, index) % rows) / rows
    cos, sin = np.cos(inner), np.sin(inner)
    middle = np.block([[cos, -sin], [sin, cos]])
    return (
        first.astype(jnp.bfloat16),
        middle.astype(jnp.bfloat16),
        (last / length).astype(jnp.bfloat16),
        np.cos(twist).astype(np.float32),
        np.sin(twist).astype(np.float32),
    )


def dot(left, right):
    return jnp.dot(left, right, preferred_element_type=jnp.float32)


def turn_kernel(signal_ref, filt_ref, out_ref):
    share = out_ref.shape[1] // 2
    for part, ref in enumerate((signal_ref, filt_ref)):
        flipped = ref[...].astype(jnp.float32).T.astype(jnp.bfloat16)
        out_ref[:, part * share : (part + 1) * share, :] = flipped.reshape(-1, share, flipped.shape[1])


def turn(signal, filt, ways):
    rows, channels = signal.shape
    share = channels // ways
    lanes = 128
    return pl.pallas_call(
        turn_kernel,
        grid=(channels // lanes,),
        in_specs=[pl.BlockSpec((rows, lanes), lambda b: (0, b))] * 2,
        out_specs=pl.BlockSpec((lanes // share, 2 * share, rows), lambda b: (b, 0, 0)),
        out_shape=jax.ShapeDtypeStruct((ways, 2 * share, rows), jnp.bfloat16),
        compiler_params=pltpu.CompilerParams(vmem_limit_bytes=8 * 2**20),
        name="turn",
    )(signal, filt)


def conv_kernel(x_ref, first_ref, middle_ref, last_ref, cos_ref, sin_ref, out_ref):
    blocks, doubled, rows = x_ref.shape
    share = doubled // 2
    half = blocks * GROUP
    cos, sin = cos_ref[...], sin_ref[...]
    for start in range(0, share, GROUP):
        parts = []
        for base in (start, share + start):
            x = x_ref[:, base : base + GROUP, :].reshape(half, rows)
            a = dot(first_ref[...], x)
            re, im = a[:half], a[half:]
            parts.append(
                jnp.concatenate([re * cos + im * sin, im * cos - re * sin], axis=1).astype(jnp.bfloat16)
            )
        spec = dot(jnp.concatenate(parts, axis=0), middle_ref[...])
        xr, xi = spec[:half, :rows], spec[:half, rows:]
        hr, hi = spec[half:, :rows], spec[half:, rows:]
        prod = jnp.concatenate([xr * hr - xi * hi, xr * hi + xi * hr], axis=1).astype(jnp.bfloat16)
        back = lax.dot_general(
            prod, middle_ref[...], (((1,), (1,)), ((), ())), preferred_element_type=jnp.float32
        )
        re, im = back[:, :rows], back[:, rows:]
        untwisted = jnp.concatenate([re * cos - im * sin, re * sin + im * cos], axis=0).astype(jnp.bfloat16)
        y = dot(last_ref[...], untwisted)
        out_ref[:, start : start + GROUP, :] = y.reshape(blocks, GROUP, rows).astype(jnp.bfloat16)


def convolve(x):
    blocks, doubled, rows = x.shape
    constants = [jnp.asarray(t) for t in tables(blocks, rows)]
    return pl.pallas_call(
        conv_kernel,
        out_shape=jax.ShapeDtypeStruct((blocks, doubled // 2, rows), jnp.bfloat16),
        compiler_params=pltpu.CompilerParams(vmem_limit_bytes=20 * 2**20),
        name="convolve",
    )(x, *constants)


def mix_kernel(conv_ref, signal_ref, gate_ref, skip_ref, out_ref):
    conv = conv_ref[...].astype(jnp.float32).T
    values = signal_ref[...].astype(jnp.float32)
    mixed = (gate_ref[...].astype(jnp.float32) * (conv + skip_ref[...] * values)).astype(jnp.bfloat16)
    width = out_ref.shape[2]
    for half in range(2):
        out_ref[half] = mixed[:, half * width : (half + 1) * width]


def mix(conv, signal, gate, skip):
    rows, channels = signal.shape
    return pl.pallas_call(
        mix_kernel,
        out_shape=jax.ShapeDtypeStruct((2, rows, channels // 2), jnp.bfloat16),
        compiler_params=pltpu.CompilerParams(vmem_limit_bytes=8 * 2**20),
        name="mix",
    )(conv, signal, gate, skip.reshape(1, channels))


def shifted(block, step):
    count = lax.axis_size("tp")
    return lax.ppermute(block, "tp", [(i, (i + step) % count) for i in range(count)])


def swapped(block):
    return lax.ppermute(block, "tp", [(i, i ^ 1) for i in range(lax.axis_size("tp"))])


def rows_of(blocks):
    count = lax.axis_size("tp")
    me = lax.axis_index("tp")
    return [2 * lax.rem((me ^ 1 if other else me) + offset + count, count) + half for other, offset, half in blocks]


def first_kernel(own, later, weights_ref, mine_ref, beside_ref, total_ref, later_ref, held_ref, sems):
    copies = []
    for j, row in enumerate(rows_of(own)):
        copies.append(pltpu.make_async_copy(weights_ref.at[row], held_ref.at[j], sems.at[j]))
    for j, row in enumerate(rows_of(later)):
        copies.append(pltpu.make_async_copy(weights_ref.at[row], later_ref.at[j], sems.at[len(own) + j]))
    for copy in copies:
        copy.start()
    left = jnp.concatenate([mine_ref[0], mine_ref[1], beside_ref[0], beside_ref[1]], axis=1)
    for copy in copies[: len(own)]:
        copy.wait()
    add_product(left, held_ref, 0, None, total_ref)
    for copy in copies[len(own) :]:
        copy.wait()


def add_product(left, weights_ref, first, total_ref, out_ref):
    width = weights_ref.shape[1]
    count = left.shape[1] // width
    lanes = 256
    for start in range(0, out_ref.shape[1], lanes):
        span = slice(start, start + lanes)
        mine = dot(left, weights_ref[first : first + count, :, span].reshape(count * width, lanes))
        if total_ref is not None:
            mine = mine + total_ref[:, span]
        out_ref[:, span] = mine.astype(out_ref.dtype)


def later_kernel(first, weights_ref, *refs):
    blocks, total_ref, out_ref = refs[:-2], refs[-2], refs[-1]
    left = jnp.concatenate([block[half] for block in blocks for half in range(block.shape[0])], axis=1)
    add_product(left, weights_ref, first, total_ref, out_ref)


VMEM = pl.BlockSpec(memory_space=pltpu.VMEM)


def cost(rows, depth, columns):
    return pl.CostEstimate(
        flops=2 * rows * depth * columns,
        bytes_accessed=2 * (rows + columns) * depth + 8 * rows * columns,
        transcendentals=0,
    )


def later_call(weights, first, blocks, total, dtype, name):
    rows, columns = total.shape
    depth = sum(block.shape[0] for block in blocks) * weights.shape[1]
    return pl.pallas_call(
        functools.partial(later_kernel, first),
        in_specs=[VMEM] * (2 + len(blocks)),
        out_specs=VMEM,
        out_shape=jax.ShapeDtypeStruct((rows, columns), dtype),
        compiler_params=pltpu.CompilerParams(vmem_limit_bytes=12 * 2**20),
        cost_estimate=cost(rows, depth, columns),
        name=name,
    )(weights, *blocks, total)


def project(mixed, w_out):
    width, columns = mixed.shape[2], w_out.shape[1]
    rows = mixed.shape[1]
    weights = w_out.reshape(-1, width, columns)
    own = [(other, 0, half) for other in (0, 1) for half in (0, 1)]
    near = [(other, offset, half) for other in (0, 1) for offset in (2, -2) for half in (0, 1)]
    far = [(other, 4, half) for other in (0, 1) for half in (0, 1)]
    later = near + far

    right, left = shifted(mixed, -2), shifted(mixed, 2)
    beside = swapped(mixed)
    total, weights = pl.pallas_call(
        functools.partial(first_kernel, own, later),
        in_specs=[pl.BlockSpec(memory_space=pl.ANY), VMEM, VMEM],
        out_specs=[VMEM, VMEM],
        out_shape=[
            jax.ShapeDtypeStruct((rows, columns), jnp.float32),
            jax.ShapeDtypeStruct((len(later), width, columns), weights.dtype),
        ],
        scratch_shapes=[
            pltpu.VMEM((len(own), width, columns), weights.dtype),
            pltpu.SemaphoreType.DMA((len(own) + len(later),)),
        ],
        compiler_params=pltpu.CompilerParams(vmem_limit_bytes=14 * 2**20),
        cost_estimate=cost(rows, len(own) * width, columns),
        name="project_own",
    )(weights, mixed, beside)
    right, left, total = lax.optimization_barrier((right, left, total))
    far_low, far_high = shifted(right[:1], -2), shifted(left[1:], 2)
    beside_right, beside_left = swapped(right), swapped(left)
    total = later_call(
        weights, 0, [right, left, beside_right, beside_left], total, jnp.float32, "project_near"
    )
    far_low, far_high, total = lax.optimization_barrier((far_low, far_high, total))
    beside_low, beside_high = swapped(far_low), swapped(far_high)
    return later_call(
        weights, len(near), [far_low, far_high, beside_low, beside_high], total, jnp.bfloat16, "project_far"
    )


def per_device(signal, gate, filt, skip, w_out):
    ways = lax.axis_size("ctx")
    rows, channels = signal.shape
    spread = lax.all_to_all(turn(signal, filt, ways), "ctx", 0, 0, tiled=True)
    conv = lax.all_to_all(convolve(spread), "ctx", 0, 0, tiled=True)
    return project(mix(conv.reshape(channels, rows), signal, gate, skip), w_out)


def solution(mesh):
    return jax.shard_map(
        per_device,
        mesh=mesh,
        in_specs=(P("ctx", "tp"), P("ctx", "tp"), P("ctx", "tp"), P("tp"), P(None, "tp")),
        out_specs=P("ctx", "tp"),
        check_vma=False,
    )
```

```python
import functools

import jax
import jax.numpy as jnp
import numpy as np
from jax import lax
from jax.experimental import pallas as pl
from jax.experimental.pallas import tpu as pltpu
from jax.sharding import PartitionSpec as P

GROUP = 16


def tables(blocks, rows):
    freq = np.arange(blocks) + 0.25
    turn = 2 * np.pi * np.outer(freq, np.arange(blocks)) / blocks
    same = np.eye(GROUP)
    outer = np.concatenate([np.kron(np.cos(turn), same), np.kron(-np.sin(turn), same)], axis=0)
    twist = np.repeat(2 * np.pi * np.outer(freq, np.arange(rows)) / (blocks * rows), GROUP, axis=0)
    index = np.arange(rows)
    inner = 2 * np.pi * (np.outer(index, index) % rows) / rows
    cos, sin = np.cos(inner), np.sin(inner)
    middle = np.block([[cos, -sin], [sin, cos]])
    return (
        outer.astype(jnp.bfloat16),
        middle.astype(jnp.bfloat16),
        np.stack([np.cos(twist), np.sin(twist)]).astype(np.float32),
    )


def dot(left, right):
    return jnp.dot(left, right, preferred_element_type=jnp.float32)


def turn_kernel(signal_ref, filt_ref, out_ref):
    ways, share, _ = out_ref.shape
    rows = signal_ref.shape[0]
    for part, ref in enumerate((signal_ref, filt_ref)):
        flipped = ref[...].astype(jnp.float32).T.astype(jnp.bfloat16)
        out_ref[:, :, part * rows : (part + 1) * rows] = flipped.reshape(ways, share, rows)


def turn(signal, filt, ways):
    rows, channels = signal.shape
    return pl.pallas_call(
        turn_kernel,
        out_shape=jax.ShapeDtypeStruct((ways, channels // ways, 2 * rows), jnp.bfloat16),
        compiler_params=pltpu.CompilerParams(vmem_limit_bytes=12 * 2**20),
        name="turn",
    )(signal, filt)


def conv_kernel(x_ref, outer_ref, middle_ref, twist_ref, out_ref):
    blocks, share, rows = out_ref.shape
    half = blocks * GROUP
    cos, sin = twist_ref[0], twist_ref[1]
    scale = 1.0 / (blocks * rows)
    for start in range(0, share, GROUP):
        parts = []
        for lane in (0, rows):
            x = x_ref[:, start : start + GROUP, lane : lane + rows].reshape(half, rows)
            a = dot(outer_ref[...], x)
            re, im = a[:half], a[half:]
            parts.append(
                jnp.concatenate([re * cos + im * sin, im * cos - re * sin], axis=1).astype(jnp.bfloat16)
            )
        spec = dot(jnp.concatenate(parts, axis=0), middle_ref[...])
        xr, xi = spec[:half, :rows], spec[:half, rows:]
        hr, hi = spec[half:, :rows], spec[half:, rows:]
        prod = jnp.concatenate([xr * hr - xi * hi, xr * hi + xi * hr], axis=1).astype(jnp.bfloat16)
        back = lax.dot_general(
            prod, middle_ref[...], (((1,), (1,)), ((), ())), preferred_element_type=jnp.float32
        )
        re, im = back[:, :rows], back[:, rows:]
        untwisted = jnp.concatenate([re * cos - im * sin, re * sin + im * cos], axis=0).astype(jnp.bfloat16)
        y = scale * lax.dot_general(
            outer_ref[...], untwisted, (((0,), (0,)), ((), ())), preferred_element_type=jnp.float32
        )
        out_ref[:, start : start + GROUP, :] = y.reshape(blocks, GROUP, rows).astype(jnp.bfloat16)


def convolve(x):
    blocks, share, rows = x.shape[0], x.shape[1], x.shape[2] // 2
    constants = [jnp.asarray(t) for t in tables(blocks, rows)]
    return pl.pallas_call(
        conv_kernel,
        out_shape=jax.ShapeDtypeStruct((blocks, share, rows), jnp.bfloat16),
        compiler_params=pltpu.CompilerParams(vmem_limit_bytes=20 * 2**20),
        name="convolve",
    )(x, *constants)


def mix_kernel(conv_ref, signal_ref, gate_ref, skip_ref, out_ref, low_ref, high_ref):
    conv = conv_ref[...].astype(jnp.float32).T
    values = signal_ref[...].astype(jnp.float32)
    mixed = (gate_ref[...].astype(jnp.float32) * (conv + skip_ref[...] * values)).astype(jnp.bfloat16)
    width = out_ref.shape[2]
    for half, half_ref in enumerate((low_ref, high_ref)):
        part = mixed[:, half * width : (half + 1) * width]
        out_ref[half] = part
        half_ref[...] = part


def mix(conv, signal, gate, skip):
    rows, channels = signal.shape
    return pl.pallas_call(
        mix_kernel,
        out_shape=[
            jax.ShapeDtypeStruct((2, rows, channels // 2), jnp.bfloat16),
            jax.ShapeDtypeStruct((rows, channels // 2), jnp.bfloat16),
            jax.ShapeDtypeStruct((rows, channels // 2), jnp.bfloat16),
        ],
        compiler_params=pltpu.CompilerParams(vmem_limit_bytes=8 * 2**20),
        name="mix",
    )(conv, signal, gate, skip.reshape(1, channels))


def shifted(block, step):
    count = lax.axis_size("tp")
    return lax.ppermute(block, "tp", [(i, (i + step) % count) for i in range(count)])


def swapped(block):
    return lax.ppermute(block, "tp", [(i, i ^ 1) for i in range(lax.axis_size("tp"))])


def rows_of(blocks):
    count = lax.axis_size("tp")
    me = lax.axis_index("tp")
    return [2 * lax.rem((me ^ 1 if other else me) + offset + count, count) + half for other, offset, half in blocks]


def first_kernel(own, later, weights_ref, mine_ref, beside_ref, total_ref, later_ref, held_ref, sems):
    copies = []
    for j, row in enumerate(rows_of(own)):
        copies.append(pltpu.make_async_copy(weights_ref.at[row], held_ref.at[j], sems.at[j]))
    for j, row in enumerate(rows_of(later)):
        copies.append(pltpu.make_async_copy(weights_ref.at[row], later_ref.at[j], sems.at[len(own) + j]))
    for copy in copies:
        copy.start()
    left = jnp.concatenate([mine_ref[0], mine_ref[1], beside_ref[0], beside_ref[1]], axis=1)
    for copy in copies[: len(own)]:
        copy.wait()
    add_product(left, held_ref, 0, None, total_ref)
    for copy in copies[len(own) :]:
        copy.wait()


def add_product(left, weights_ref, first, total_ref, out_ref):
    width = weights_ref.shape[1]
    count = left.shape[1] // width
    lanes = 256
    for start in range(0, out_ref.shape[1], lanes):
        span = slice(start, start + lanes)
        mine = dot(left, weights_ref[first : first + count, :, span].reshape(count * width, lanes))
        if total_ref is not None:
            mine = mine + total_ref[:, span]
        out_ref[:, span] = mine.astype(out_ref.dtype)


def later_kernel(first, weights_ref, *refs):
    blocks, total_ref, out_ref = refs[:-2], refs[-2], refs[-1]
    left = jnp.concatenate([block[...] for block in blocks], axis=1)
    add_product(left, weights_ref, first, total_ref, out_ref)


VMEM = pl.BlockSpec(memory_space=pltpu.VMEM)


def cost(rows, depth, columns):
    return pl.CostEstimate(
        flops=2 * rows * depth * columns,
        bytes_accessed=2 * (rows + columns) * depth + 8 * rows * columns,
        transcendentals=0,
    )


def later_call(weights, first, blocks, total, dtype, name):
    rows, columns = total.shape
    depth = len(blocks) * weights.shape[1]
    return pl.pallas_call(
        functools.partial(later_kernel, first),
        in_specs=[VMEM] * (2 + len(blocks)),
        out_specs=VMEM,
        out_shape=jax.ShapeDtypeStruct((rows, columns), dtype),
        compiler_params=pltpu.CompilerParams(vmem_limit_bytes=12 * 2**20),
        cost_estimate=cost(rows, depth, columns),
        name=name,
    )(weights, *blocks, total)


def project(mixed, low, high, w_out):
    width, columns = mixed.shape[2], w_out.shape[1]
    rows = mixed.shape[1]
    weights = w_out.reshape(-1, width, columns)
    own = [(other, 0, half) for other in (0, 1) for half in (0, 1)]
    near = [(other, offset, half) for other in (0, 1) for offset in (2, -2) for half in (0, 1)]
    far = [(other, 4, half) for other in (0, 1) for half in (0, 1)]
    later = near + far

    right_low, left_high = shifted(low, -2), shifted(high, 2)
    beside = swapped(mixed)
    low, high, beside = lax.optimization_barrier((low, high, beside))
    right_high, left_low = shifted(high, -2), shifted(low, 2)
    total, weights = pl.pallas_call(
        functools.partial(first_kernel, own, later),
        in_specs=[pl.BlockSpec(memory_space=pl.ANY), VMEM, VMEM],
        out_specs=[VMEM, VMEM],
        out_shape=[
            jax.ShapeDtypeStruct((rows, columns), jnp.float32),
            jax.ShapeDtypeStruct((len(later), width, columns), weights.dtype),
        ],
        scratch_shapes=[
            pltpu.VMEM((len(own), width, columns), weights.dtype),
            pltpu.SemaphoreType.DMA((len(own) + len(later),)),
        ],
        compiler_params=pltpu.CompilerParams(vmem_limit_bytes=44 * 2**20),
        cost_estimate=cost(rows, len(own) * width, columns),
        name="project_own",
    )(weights, mixed, beside)
    right_low, left_high, total = lax.optimization_barrier((right_low, left_high, total))
    far_low, far_high = shifted(right_low, -2), shifted(left_high, 2)
    near_blocks = [right_low, right_high, left_low, left_high]
    near_blocks += [swapped(block) for block in near_blocks]
    *near_blocks, far_low, far_high, total = lax.optimization_barrier((*near_blocks, far_low, far_high, total))
    beside_low, beside_high = swapped(far_low), swapped(far_high)
    total = later_call(weights, 0, [*near_blocks, far_low, far_high], total, jnp.float32, "project_near")
    return later_call(weights, len(near) + 2, [beside_low, beside_high], total, jnp.bfloat16, "project_last")


def per_device(signal, gate, filt, skip, w_out):
    ways = lax.axis_size("ctx")
    rows, channels = signal.shape
    spread = lax.all_to_all(turn(signal, filt, ways), "ctx", 0, 0, tiled=True)
    conv = lax.all_to_all(convolve(spread), "ctx", 0, 0, tiled=True)
    return project(*mix(conv.reshape(channels, rows), signal, gate, skip), w_out)


def solution(mesh):
    return jax.shard_map(
        per_device,
        mesh=mesh,
        in_specs=(P("ctx", "tp"), P("ctx", "tp"), P("ctx", "tp"), P("tp"), P(None, "tp")),
        out_specs=P("ctx", "tp"),
        check_vma=False,
    )
```

```python
import functools

import jax
import jax.numpy as jnp
import numpy as np
from jax import lax
from jax.experimental import pallas as pl
from jax.experimental.pallas import tpu as pltpu
from jax.sharding import PartitionSpec as P

GROUP = 16


def tables(blocks, rows):
    coarse, fine = 2 * blocks, rows // 2
    freq = np.arange(coarse) + 0.25
    turn = 2 * np.pi * np.outer(freq, np.arange(coarse)) / coarse
    turn = np.concatenate([turn[:, 0::2], turn[:, 1::2]], axis=1)
    same = np.eye(GROUP)
    outer = np.concatenate([np.kron(np.cos(turn), same), np.kron(-np.sin(turn), same)], axis=0)
    twist = np.repeat(2 * np.pi * np.outer(freq, np.arange(fine)) / (coarse * fine), GROUP, axis=0)
    index = np.arange(fine)
    inner = 2 * np.pi * (np.outer(index, index) % fine) / fine
    cos, sin = np.cos(inner), np.sin(inner)
    middle = np.block([[cos, -sin], [sin, cos]])
    return (
        np.concatenate([outer, middle], axis=0).astype(jnp.bfloat16),
        np.concatenate([np.cos(twist), np.sin(twist)], axis=1).astype(np.float32),
    )


def dot(left, right):
    return jnp.dot(left, right, preferred_element_type=jnp.float32)


def turn_kernel(signal_ref, filt_ref, out_ref):
    ways, share, _ = out_ref.shape
    rows = signal_ref.shape[0]
    for part, ref in enumerate((signal_ref, filt_ref)):
        flipped = ref[...].astype(jnp.float32).T.astype(jnp.bfloat16)
        out_ref[:, :, part * rows : (part + 1) * rows] = flipped.reshape(ways, share, rows)


def turn(signal, filt, ways):
    rows, channels = signal.shape
    return pl.pallas_call(
        turn_kernel,
        out_shape=jax.ShapeDtypeStruct((ways, channels // ways, 2 * rows), jnp.bfloat16),
        compiler_params=pltpu.CompilerParams(vmem_limit_bytes=12 * 2**20),
        name="turn",
    )(signal, filt)


def conv_kernel(x_ref, table_ref, twist_ref, out_ref):
    blocks, share, rows = out_ref.shape
    fine = rows // 2
    half = 2 * blocks * GROUP
    cos, sin = twist_ref[:, :fine], twist_ref[:, fine:]
    outer_ref, middle_ref = table_ref.at[: 2 * half], table_ref.at[2 * half :]
    scale = 1.0 / (blocks * rows)
    for start in range(0, share, GROUP):
        group = slice(start, start + GROUP)
        parts = []
        for lane in (0, rows):
            spans = [slice(lane, lane + fine), slice(lane + fine, lane + rows)]
            x = jnp.concatenate([x_ref[:, group, span].reshape(blocks * GROUP, fine) for span in spans], axis=0)
            a = dot(outer_ref[...], x)
            re, im = a[:half], a[half:]
            parts.append(
                jnp.concatenate([re * cos + im * sin, im * cos - re * sin], axis=1).astype(jnp.bfloat16)
            )
        spec = dot(jnp.concatenate(parts, axis=0), middle_ref[...])
        xr, xi = spec[:half, :fine], spec[:half, fine:]
        hr, hi = spec[half:, :fine], spec[half:, fine:]
        prod = jnp.concatenate([xr * hr - xi * hi, xr * hi + xi * hr], axis=1).astype(jnp.bfloat16)
        back = lax.dot_general(
            prod, middle_ref[...], (((1,), (1,)), ((), ())), preferred_element_type=jnp.float32
        )
        re, im = back[:, :fine], back[:, fine:]
        untwisted = jnp.concatenate([re * cos - im * sin, re * sin + im * cos], axis=0).astype(jnp.bfloat16)
        y = scale * lax.dot_general(
            outer_ref[...], untwisted, (((0,), (0,)), ((), ())), preferred_element_type=jnp.float32
        )
        y = y.astype(jnp.bfloat16).reshape(2, blocks, GROUP, fine)
        out_ref[:, group, :fine] = y[0]
        out_ref[:, group, fine:] = y[1]


def convolve(x):
    blocks, share, rows = x.shape[0], x.shape[1], x.shape[2] // 2
    constants = [jnp.asarray(t) for t in tables(blocks, rows)]
    return pl.pallas_call(
        conv_kernel,
        out_shape=jax.ShapeDtypeStruct((blocks, share, rows), jnp.bfloat16),
        compiler_params=pltpu.CompilerParams(vmem_limit_bytes=20 * 2**20),
        name="convolve",
    )(x, *constants)


def mix_kernel(conv_ref, signal_ref, gate_ref, skip_ref, out_ref, low_ref, high_ref):
    conv = conv_ref[...].astype(jnp.float32).T
    values = signal_ref[...].astype(jnp.float32)
    mixed = (gate_ref[...].astype(jnp.float32) * (conv + skip_ref[...] * values)).astype(jnp.bfloat16)
    width = out_ref.shape[2]
    for half, half_ref in enumerate((low_ref, high_ref)):
        part = mixed[:, half * width : (half + 1) * width]
        out_ref[half] = part
        half_ref[...] = part


def mix(conv, signal, gate, skip):
    rows, channels = signal.shape
    return pl.pallas_call(
        mix_kernel,
        out_shape=[
            jax.ShapeDtypeStruct((2, rows, channels // 2), jnp.bfloat16),
            jax.ShapeDtypeStruct((rows, channels // 2), jnp.bfloat16),
            jax.ShapeDtypeStruct((rows, channels // 2), jnp.bfloat16),
        ],
        compiler_params=pltpu.CompilerParams(vmem_limit_bytes=8 * 2**20),
        name="mix",
    )(conv, signal, gate, skip.reshape(1, channels))


def shifted(block, step):
    count = lax.axis_size("tp")
    return lax.ppermute(block, "tp", [(i, (i + step) % count) for i in range(count)])


def swapped(block):
    return lax.ppermute(block, "tp", [(i, i ^ 1) for i in range(lax.axis_size("tp"))])


def rows_of(blocks):
    count = lax.axis_size("tp")
    me = lax.axis_index("tp")
    return [2 * lax.rem((me ^ 1 if other else me) + offset + count, count) + half for other, offset, half in blocks]


def first_kernel(own, later, weights_ref, mine_ref, beside_ref, total_ref, later_ref, held_ref, sems):
    copies = []
    for j, row in enumerate(rows_of(own)):
        copies.append(pltpu.make_async_copy(weights_ref.at[row], held_ref.at[j], sems.at[j]))
    for j, row in enumerate(rows_of(later)):
        copies.append(pltpu.make_async_copy(weights_ref.at[row], later_ref.at[j], sems.at[len(own) + j]))
    for copy in copies:
        copy.start()
    left = jnp.concatenate([mine_ref[0], mine_ref[1], beside_ref[0], beside_ref[1]], axis=1)
    for copy in copies[: len(own)]:
        copy.wait()
    add_product(left, held_ref, 0, None, total_ref)
    for copy in copies[len(own) :]:
        copy.wait()


def add_product(left, weights_ref, first, total_ref, out_ref):
    width = weights_ref.shape[1]
    count = left.shape[1] // width
    lanes = 256
    for start in range(0, out_ref.shape[1], lanes):
        span = slice(start, start + lanes)
        mine = dot(left, weights_ref[first : first + count, :, span].reshape(count * width, lanes))
        if total_ref is not None:
            mine = mine + total_ref[:, span]
        out_ref[:, span] = mine.astype(out_ref.dtype)


def later_kernel(first, weights_ref, *refs):
    blocks, total_ref, out_ref = refs[:-2], refs[-2], refs[-1]
    left = jnp.concatenate([block[...] for block in blocks], axis=1)
    add_product(left, weights_ref, first, total_ref, out_ref)


def last_kernel(first, weights_ref, *refs):
    blocks, total_ref, out_ref, held_ref, sems = refs[:-4], refs[-4], refs[-3], refs[-2], refs[-1]
    left = jnp.concatenate([block[...] for block in blocks], axis=1)
    count, width = len(blocks), weights_ref.shape[1]
    lanes = held_ref.shape[2]
    copies = []
    for step in range(held_ref.shape[0]):
        span = slice(step * lanes, (step + 1) * lanes)
        mine = dot(left, weights_ref[first : first + count, :, span].reshape(count * width, lanes))
        held_ref[step] = (mine + total_ref[:, span]).astype(out_ref.dtype)
        copies.append(pltpu.make_async_copy(held_ref.at[step], out_ref.at[:, span], sems.at[step]))
        copies[-1].start()
    for copy in copies:
        copy.wait()


def last_call(weights, first, blocks, total, dtype):
    rows, columns = total.shape
    steps = 4
    return pl.pallas_call(
        functools.partial(last_kernel, first),
        in_specs=[VMEM] * (2 + len(blocks)),
        out_specs=pl.BlockSpec(memory_space=pl.ANY),
        out_shape=jax.ShapeDtypeStruct((rows, columns), dtype),
        scratch_shapes=[
            pltpu.VMEM((steps, rows, columns // steps), dtype),
            pltpu.SemaphoreType.DMA((steps,)),
        ],
        compiler_params=pltpu.CompilerParams(vmem_limit_bytes=12 * 2**20),
        name="project_last",
    )(weights, *blocks, total)


VMEM = pl.BlockSpec(memory_space=pltpu.VMEM)


def cost(rows, depth, columns):
    return pl.CostEstimate(
        flops=2 * rows * depth * columns,
        bytes_accessed=2 * (rows + columns) * depth + 8 * rows * columns,
        transcendentals=0,
    )


def later_call(weights, first, blocks, total, dtype, name):
    rows, columns = total.shape
    depth = len(blocks) * weights.shape[1]
    return pl.pallas_call(
        functools.partial(later_kernel, first),
        in_specs=[VMEM] * (2 + len(blocks)),
        out_specs=VMEM,
        out_shape=jax.ShapeDtypeStruct((rows, columns), dtype),
        compiler_params=pltpu.CompilerParams(vmem_limit_bytes=12 * 2**20),
        cost_estimate=cost(rows, depth, columns),
        name=name,
    )(weights, *blocks, total)


def project(mixed, low, high, w_out):
    width, columns = mixed.shape[2], w_out.shape[1]
    rows = mixed.shape[1]
    weights = w_out.reshape(-1, width, columns)
    own = [(other, 0, half) for other in (0, 1) for half in (0, 1)]
    near = [(other, offset, half) for other in (0, 1) for offset in (2, -2) for half in (0, 1)]
    far = [(other, 4, half) for other in (0, 1) for half in (0, 1)]
    later = near + far

    right_low, left_high = shifted(low, -2), shifted(high, 2)
    beside = swapped(mixed)
    low, high, beside = lax.optimization_barrier((low, high, beside))
    right_high, left_low = shifted(high, -2), shifted(low, 2)
    total, weights = pl.pallas_call(
        functools.partial(first_kernel, own, later),
        in_specs=[pl.BlockSpec(memory_space=pl.ANY), VMEM, VMEM],
        out_specs=[VMEM, VMEM],
        out_shape=[
            jax.ShapeDtypeStruct((rows, columns), jnp.float32),
            jax.ShapeDtypeStruct((len(later), width, columns), weights.dtype),
        ],
        scratch_shapes=[
            pltpu.VMEM((len(own), width, columns), weights.dtype),
            pltpu.SemaphoreType.DMA((len(own) + len(later),)),
        ],
        compiler_params=pltpu.CompilerParams(vmem_limit_bytes=44 * 2**20),
        cost_estimate=cost(rows, len(own) * width, columns),
        name="project_own",
    )(weights, mixed, beside)
    right_low, left_high, total = lax.optimization_barrier((right_low, left_high, total))
    far_low, far_high = shifted(right_low, -2), shifted(left_high, 2)
    near_blocks = [right_low, right_high, left_low, left_high]
    near_blocks += [swapped(block) for block in near_blocks]
    *near_blocks, far_low, far_high, total = lax.optimization_barrier((*near_blocks, far_low, far_high, total))
    beside_low, beside_high = swapped(far_low), swapped(far_high)
    total = later_call(weights, 0, [*near_blocks, far_low, far_high], total, jnp.float32, "project_near")
    return last_call(weights, len(near) + 2, [beside_low, beside_high], total, jnp.bfloat16)


def per_device(signal, gate, filt, skip, w_out):
    ways = lax.axis_size("ctx")
    rows, channels = signal.shape
    spread = lax.all_to_all(turn(signal, filt, ways), "ctx", 0, 0, tiled=True)
    conv = lax.all_to_all(convolve(spread), "ctx", 0, 0, tiled=True)
    return project(*mix(conv.reshape(channels, rows), signal, gate, skip), w_out)


def solution(mesh):
    return jax.shard_map(
        per_device,
        mesh=mesh,
        in_specs=(P("ctx", "tp"), P("ctx", "tp"), P("ctx", "tp"), P("tp"), P(None, "tp")),
        out_specs=P("ctx", "tp"),
        check_vma=False,
    )
```

```python
import functools

import jax
import jax.numpy as jnp
import numpy as np
from jax import lax
from jax.experimental import pallas as pl
from jax.experimental.pallas import tpu as pltpu
from jax.sharding import PartitionSpec as P

GROUP = 16


def tables(blocks, rows):
    coarse, fine = 2 * blocks, rows // 2
    freq = np.arange(coarse) + 0.25
    turn = 2 * np.pi * np.outer(freq, np.arange(coarse)) / coarse
    turn = np.concatenate([turn[:, 0::2], turn[:, 1::2]], axis=1)
    same = np.eye(GROUP)
    outer = np.concatenate([np.kron(np.cos(turn), same), np.kron(-np.sin(turn), same)], axis=0)
    twist = np.repeat(2 * np.pi * np.outer(freq, np.arange(fine)) / (coarse * fine), GROUP, axis=0)
    index = np.arange(fine)
    inner = 2 * np.pi * (np.outer(index, index) % fine) / fine
    cos, sin = np.cos(inner), np.sin(inner)
    middle = np.block([[cos, -sin], [sin, cos]])
    return (
        np.concatenate([outer, middle], axis=0).astype(jnp.bfloat16),
        np.concatenate([np.cos(twist), np.sin(twist)], axis=1).astype(np.float32),
    )


def dot(left, right):
    return jnp.dot(left, right, preferred_element_type=jnp.float32)


def turn_kernel(signal_ref, filt_ref, out_ref):
    ways, share, _ = out_ref.shape
    rows = signal_ref.shape[0]
    for part, ref in enumerate((signal_ref, filt_ref)):
        flipped = ref[...].astype(jnp.float32).T.astype(jnp.bfloat16)
        out_ref[:, :, part * rows : (part + 1) * rows] = flipped.reshape(ways, share, rows)


def turn(signal, filt, ways):
    rows, channels = signal.shape
    return pl.pallas_call(
        turn_kernel,
        out_shape=jax.ShapeDtypeStruct((ways, channels // ways, 2 * rows), jnp.bfloat16),
        compiler_params=pltpu.CompilerParams(vmem_limit_bytes=12 * 2**20),
        name="turn",
    )(signal, filt)


def conv_kernel(x_ref, table_ref, twist_ref, out_ref):
    blocks, share, rows = out_ref.shape
    fine = rows // 2
    half = 2 * blocks * GROUP
    cos, sin = twist_ref[:, :fine], twist_ref[:, fine:]
    outer_ref, middle_ref = table_ref.at[: 2 * half], table_ref.at[2 * half :]
    scale = 1.0 / (blocks * rows)
    for start in range(0, share, GROUP):
        group = slice(start, start + GROUP)
        parts = []
        for lane in (0, rows):
            spans = [slice(lane, lane + fine), slice(lane + fine, lane + rows)]
            x = jnp.concatenate([x_ref[:, group, span].reshape(blocks * GROUP, fine) for span in spans], axis=0)
            a = dot(outer_ref[...], x)
            re, im = a[:half], a[half:]
            parts.append(
                jnp.concatenate([re * cos + im * sin, im * cos - re * sin], axis=1).astype(jnp.bfloat16)
            )
        spec = dot(jnp.concatenate(parts, axis=0), middle_ref[...])
        xr, xi = spec[:half, :fine], spec[:half, fine:]
        hr, hi = spec[half:, :fine], spec[half:, fine:]
        prod = jnp.concatenate([xr * hr - xi * hi, xr * hi + xi * hr], axis=1).astype(jnp.bfloat16)
        back = lax.dot_general(
            prod, middle_ref[...], (((1,), (1,)), ((), ())), preferred_element_type=jnp.float32
        )
        re, im = back[:, :fine], back[:, fine:]
        untwisted = jnp.concatenate([re * cos - im * sin, re * sin + im * cos], axis=0).astype(jnp.bfloat16)
        y = scale * lax.dot_general(
            outer_ref[...], untwisted, (((0,), (0,)), ((), ())), preferred_element_type=jnp.float32
        )
        y = y.astype(jnp.bfloat16).reshape(2, blocks, GROUP, fine)
        out_ref[:, group, :fine] = y[0]
        out_ref[:, group, fine:] = y[1]


def convolve(x):
    blocks, share, rows = x.shape[0], x.shape[1], x.shape[2] // 2
    constants = [jnp.asarray(t) for t in tables(blocks, rows)]
    return pl.pallas_call(
        conv_kernel,
        out_shape=jax.ShapeDtypeStruct((blocks, share, rows), jnp.bfloat16),
        compiler_params=pltpu.CompilerParams(vmem_limit_bytes=20 * 2**20),
        name="convolve",
    )(x, *constants)


def mix_kernel(conv_ref, signal_ref, gate_ref, skip_ref, out_ref):
    conv = conv_ref[...].astype(jnp.float32).T
    values = signal_ref[...].astype(jnp.float32)
    out_ref[...] = (gate_ref[...].astype(jnp.float32) * (conv + skip_ref[...] * values)).astype(jnp.bfloat16)


def mix(conv, signal, gate, skip):
    rows, channels = signal.shape
    return pl.pallas_call(
        mix_kernel,
        out_shape=jax.ShapeDtypeStruct((rows, channels), jnp.bfloat16),
        compiler_params=pltpu.CompilerParams(vmem_limit_bytes=8 * 2**20),
        name="mix",
    )(conv, signal, gate, skip.reshape(1, channels))


def toward(device, step):
    count = lax.axis_size("tp")
    return (device + 2 * step * (1 - 2 * (device % 2)) + count) % count


def shifted(block, step):
    return lax.ppermute(block, "tp", [(i, toward(i, step)) for i in range(lax.axis_size("tp"))])


def swapped(block):
    return lax.ppermute(block, "tp", [(i, i ^ 1) for i in range(lax.axis_size("tp"))])


def rows_of(blocks):
    me = lax.axis_index("tp")
    return [toward(me ^ 1 if other else me, step) for other, step in blocks]


def first_kernel(own, later, weights_ref, mine_ref, beside_ref, total_ref, later_ref, held_ref, sems):
    copies = []
    for j, row in enumerate(rows_of(own)):
        copies.append(pltpu.make_async_copy(weights_ref.at[row], held_ref.at[j], sems.at[j]))
    for j, row in enumerate(rows_of(later)):
        copies.append(pltpu.make_async_copy(weights_ref.at[row], later_ref.at[j], sems.at[len(own) + j]))
    for copy in copies:
        copy.start()
    left = jnp.concatenate([mine_ref[...], beside_ref[...]], axis=1)
    for copy in copies[: len(own)]:
        copy.wait()
    add_product(left, held_ref, 0, None, total_ref)
    for copy in copies[len(own) :]:
        copy.wait()


def add_product(left, weights_ref, first, total_ref, out_ref):
    width = weights_ref.shape[1]
    count = left.shape[1] // width
    lanes = 256
    for start in range(0, out_ref.shape[1], lanes):
        span = slice(start, start + lanes)
        mine = dot(left, weights_ref[first : first + count, :, span].reshape(count * width, lanes))
        if total_ref is not None:
            mine = mine + total_ref[:, span]
        out_ref[:, span] = mine.astype(out_ref.dtype)


def later_kernel(first, weights_ref, *refs):
    blocks, total_ref, out_ref = refs[:-2], refs[-2], refs[-1]
    left = jnp.concatenate([block[...] for block in blocks], axis=1)
    add_product(left, weights_ref, first, total_ref, out_ref)


def last_kernel(first, weights_ref, *refs):
    blocks, total_ref, out_ref, held_ref, sems = refs[:-4], refs[-4], refs[-3], refs[-2], refs[-1]
    left = jnp.concatenate([block[...] for block in blocks], axis=1)
    count, width = len(blocks), weights_ref.shape[1]
    lanes = held_ref.shape[2]
    copies = []
    for step in range(held_ref.shape[0]):
        span = slice(step * lanes, (step + 1) * lanes)
        mine = dot(left, weights_ref[first : first + count, :, span].reshape(count * width, lanes))
        held_ref[step] = (mine + total_ref[:, span]).astype(out_ref.dtype)
        copies.append(pltpu.make_async_copy(held_ref.at[step], out_ref.at[:, span], sems.at[step]))
        copies[-1].start()
    for copy in copies:
        copy.wait()


def last_call(weights, first, blocks, total, dtype):
    rows, columns = total.shape
    steps = 4
    return pl.pallas_call(
        functools.partial(last_kernel, first),
        in_specs=[VMEM] * (2 + len(blocks)),
        out_specs=pl.BlockSpec(memory_space=pl.ANY),
        out_shape=jax.ShapeDtypeStruct((rows, columns), dtype),
        scratch_shapes=[
            pltpu.VMEM((steps, rows, columns // steps), dtype),
            pltpu.SemaphoreType.DMA((steps,)),
        ],
        compiler_params=pltpu.CompilerParams(vmem_limit_bytes=12 * 2**20),
        name="project_last",
    )(weights, *blocks, total)


VMEM = pl.BlockSpec(memory_space=pltpu.VMEM)


def cost(rows, depth, columns):
    return pl.CostEstimate(
        flops=2 * rows * depth * columns,
        bytes_accessed=2 * (rows + columns) * depth + 8 * rows * columns,
        transcendentals=0,
    )


def later_call(weights, first, blocks, total, dtype, name):
    rows, columns = total.shape
    depth = len(blocks) * weights.shape[1]
    return pl.pallas_call(
        functools.partial(later_kernel, first),
        in_specs=[VMEM] * (2 + len(blocks)),
        out_specs=VMEM,
        out_shape=jax.ShapeDtypeStruct((rows, columns), dtype),
        compiler_params=pltpu.CompilerParams(vmem_limit_bytes=12 * 2**20),
        cost_estimate=cost(rows, depth, columns),
        name=name,
    )(weights, *blocks, total)


def project(mixed, w_out):
    rows, width = mixed.shape
    columns = w_out.shape[1]
    weights = w_out.reshape(-1, width, columns)
    own = [(0, 0), (1, 0)]
    later = [(0, 1), (1, 1), (0, -1), (1, -1), (0, 2), (1, 2)]

    ahead = shifted(mixed, -1)
    beside = swapped(mixed)
    total, weights = pl.pallas_call(
        functools.partial(first_kernel, own, later),
        in_specs=[pl.BlockSpec(memory_space=pl.ANY), VMEM, VMEM],
        out_specs=[VMEM, VMEM],
        out_shape=[
            jax.ShapeDtypeStruct((rows, columns), jnp.float32),
            jax.ShapeDtypeStruct((len(later), width, columns), weights.dtype),
        ],
        scratch_shapes=[
            pltpu.VMEM((len(own), width, columns), weights.dtype),
            pltpu.SemaphoreType.DMA((len(own) + len(later),)),
        ],
        compiler_params=pltpu.CompilerParams(vmem_limit_bytes=44 * 2**20),
        cost_estimate=cost(rows, len(own) * width, columns),
        name="project_own",
    )(weights, mixed, beside)
    mixed, total = lax.optimization_barrier((mixed, total))
    behind = shifted(mixed, 1)
    ahead, total = lax.optimization_barrier((ahead, total))
    far = shifted(ahead, -1)
    total = later_call(weights, 0, [ahead, swapped(ahead)], total, jnp.float32, "project_middle")
    near_blocks = [behind, swapped(behind)]
    *near_blocks, far, total = lax.optimization_barrier((*near_blocks, far, total))
    beside_far = swapped(far)
    total = later_call(weights, 2, [*near_blocks, far], total, jnp.float32, "project_near")
    return last_call(weights, len(later) - 1, [beside_far], total, jnp.bfloat16)


def per_device(signal, gate, filt, skip, w_out):
    ways = lax.axis_size("ctx")
    rows, channels = signal.shape
    spread = lax.all_to_all(turn(signal, filt, ways), "ctx", 0, 0, tiled=True)
    conv = lax.all_to_all(convolve(spread), "ctx", 0, 0, tiled=True)
    return project(mix(conv.reshape(channels, rows), signal, gate, skip), w_out)


def solution(mesh):
    return jax.shard_map(
        per_device,
        mesh=mesh,
        in_specs=(P("ctx", "tp"), P("ctx", "tp"), P("ctx", "tp"), P("tp"), P(None, "tp")),
        out_specs=P("ctx", "tp"),
        check_vma=False,
    )
```

```python
import functools

import jax
import jax.numpy as jnp
import numpy as np
from jax import lax
from jax.experimental import pallas as pl
from jax.experimental.pallas import tpu as pltpu
from jax.sharding import PartitionSpec as P

GROUP = 16


def tables(blocks, rows):
    coarse, fine = 2 * blocks, rows // 2
    freq = np.arange(coarse) + 0.25
    turn = 2 * np.pi * np.outer(freq, np.arange(coarse)) / coarse
    turn = np.concatenate([turn[:, 0::2], turn[:, 1::2]], axis=1)
    same = np.eye(GROUP)
    outer = np.concatenate([np.kron(np.cos(turn), same), np.kron(-np.sin(turn), same)], axis=0)
    twist = np.repeat(2 * np.pi * np.outer(freq, np.arange(fine)) / (coarse * fine), GROUP, axis=0)
    index = np.arange(fine)
    inner = 2 * np.pi * (np.outer(index, index) % fine) / fine
    cos, sin = np.cos(inner), np.sin(inner)
    middle = np.block([[cos, -sin], [sin, cos]])
    return (
        np.concatenate([outer, middle], axis=0).astype(jnp.bfloat16),
        np.concatenate([np.cos(twist), np.sin(twist)], axis=1).astype(np.float32),
    )


def dot(left, right):
    return jnp.dot(left, right, preferred_element_type=jnp.float32)


def turn_kernel(signal_ref, filt_ref, out_ref):
    ways, share, _ = out_ref.shape
    rows = signal_ref.shape[0]
    for part, ref in enumerate((signal_ref, filt_ref)):
        flipped = ref[...].astype(jnp.float32).T.astype(jnp.bfloat16)
        out_ref[:, :, part * rows : (part + 1) * rows] = flipped.reshape(ways, share, rows)


def turn(signal, filt, ways):
    rows, channels = signal.shape
    return pl.pallas_call(
        turn_kernel,
        out_shape=jax.ShapeDtypeStruct((ways, channels // ways, 2 * rows), jnp.bfloat16),
        compiler_params=pltpu.CompilerParams(vmem_limit_bytes=12 * 2**20),
        name="turn",
    )(signal, filt)


def conv_kernel(x_ref, table_ref, twist_ref, out_ref):
    blocks, share, rows = out_ref.shape
    fine = rows // 2
    half = 2 * blocks * GROUP
    cos, sin = twist_ref[:, :fine], twist_ref[:, fine:]
    outer_ref, middle_ref = table_ref.at[: 2 * half], table_ref.at[2 * half :]
    scale = 1.0 / (blocks * rows)
    groups = [slice(start, start + GROUP) for start in range(0, share, GROUP)]

    def enter(group, lane):
        spans = [slice(lane, lane + fine), slice(lane + fine, lane + rows)]
        x = jnp.concatenate([x_ref[:, group, span].reshape(blocks * GROUP, fine) for span in spans], axis=0)
        return dot(outer_ref[...], x)

    def twist(a):
        re, im = a[:half], a[half:]
        return jnp.concatenate([re * cos + im * sin, im * cos - re * sin], axis=1).astype(jnp.bfloat16)

    def product(spec_x, spec_h):
        xr, xi, hr, hi = spec_x[:, :fine], spec_x[:, fine:], spec_h[:, :fine], spec_h[:, fine:]
        return jnp.concatenate([xr * hr - xi * hi, xr * hi + xi * hr], axis=1).astype(jnp.bfloat16)

    def back(prod):
        return lax.dot_general(
            prod, middle_ref[...], (((1,), (1,)), ((), ())), preferred_element_type=jnp.float32
        )

    def untwist(b):
        re, im = b[:, :fine], b[:, fine:]
        return jnp.concatenate([re * cos - im * sin, re * sin + im * cos], axis=0).astype(jnp.bfloat16)

    def leave(group, turned):
        y = scale * lax.dot_general(
            outer_ref[...], turned, (((0,), (0,)), ((), ())), preferred_element_type=jnp.float32
        )
        y = y.astype(jnp.bfloat16).reshape(2, blocks, GROUP, fine)
        out_ref[:, group, :fine] = y[0]
        out_ref[:, group, fine:] = y[1]

    entered = [[enter(group, lane) for lane in (0, rows)] for group in groups]
    spectra = [[dot(twist(a), middle_ref[...]) for a in pair] for pair in entered]
    returned = [back(product(*pair)) for pair in spectra]
    for group, b in zip(groups, returned):
        leave(group, untwist(b))


def convolve(x):
    blocks, share, rows = x.shape[0], x.shape[1], x.shape[2] // 2
    constants = [jnp.asarray(t) for t in tables(blocks, rows)]
    return pl.pallas_call(
        conv_kernel,
        out_shape=jax.ShapeDtypeStruct((blocks, share, rows), jnp.bfloat16),
        compiler_params=pltpu.CompilerParams(vmem_limit_bytes=20 * 2**20),
        name="convolve",
    )(x, *constants)


def mix_kernel(conv_ref, signal_ref, gate_ref, skip_ref, out_ref):
    conv = conv_ref[...].astype(jnp.float32).T
    values = signal_ref[...].astype(jnp.float32)
    out_ref[...] = (gate_ref[...].astype(jnp.float32) * (conv + skip_ref[...] * values)).astype(jnp.bfloat16)


def mix(conv, signal, gate, skip):
    rows, channels = signal.shape
    return pl.pallas_call(
        mix_kernel,
        out_shape=jax.ShapeDtypeStruct((rows, channels), jnp.bfloat16),
        compiler_params=pltpu.CompilerParams(vmem_limit_bytes=8 * 2**20),
        name="mix",
    )(conv, signal, gate, skip.reshape(1, channels))


def toward(device, step):
    count = lax.axis_size("tp")
    return (device + 2 * step * (1 - 2 * (device % 2)) + count) % count


def shifted(block, step):
    return lax.ppermute(block, "tp", [(i, toward(i, step)) for i in range(lax.axis_size("tp"))])


def swapped(block):
    return lax.ppermute(block, "tp", [(i, i ^ 1) for i in range(lax.axis_size("tp"))])


def rows_of(blocks):
    me = lax.axis_index("tp")
    return [toward(me ^ 1 if other else me, step) for other, step in blocks]


def first_kernel(own, later, weights_ref, mine_ref, beside_ref, total_ref, later_ref, held_ref, sems):
    copies = []
    for j, row in enumerate(rows_of(own)):
        copies.append(pltpu.make_async_copy(weights_ref.at[row], held_ref.at[j], sems.at[j]))
    for j, row in enumerate(rows_of(later)):
        copies.append(pltpu.make_async_copy(weights_ref.at[row], later_ref.at[j], sems.at[len(own) + j]))
    for copy in copies:
        copy.start()
    left = jnp.concatenate([mine_ref[...], beside_ref[...]], axis=1)
    for copy in copies[: len(own)]:
        copy.wait()
    add_product(left, held_ref, 0, None, total_ref)
    for copy in copies[len(own) :]:
        copy.wait()


def add_product(left, weights_ref, first, total_ref, out_ref):
    width = weights_ref.shape[1]
    count = left.shape[1] // width
    lanes = 256
    for start in range(0, out_ref.shape[1], lanes):
        span = slice(start, start + lanes)
        mine = dot(left, weights_ref[first : first + count, :, span].reshape(count * width, lanes))
        if total_ref is not None:
            mine = mine + total_ref[:, span]
        out_ref[:, span] = mine.astype(out_ref.dtype)


def later_kernel(first, weights_ref, *refs):
    blocks, total_ref, out_ref = refs[:-2], refs[-2], refs[-1]
    left = jnp.concatenate([block[...] for block in blocks], axis=1)
    add_product(left, weights_ref, first, total_ref, out_ref)


def last_kernel(first, weights_ref, *refs):
    blocks, total_ref, out_ref, held_ref, sems = refs[:-4], refs[-4], refs[-3], refs[-2], refs[-1]
    left = jnp.concatenate([block[...] for block in blocks], axis=1)
    count, width = len(blocks), weights_ref.shape[1]
    lanes = held_ref.shape[2]
    copies = []
    for step in range(held_ref.shape[0]):
        span = slice(step * lanes, (step + 1) * lanes)
        mine = dot(left, weights_ref[first : first + count, :, span].reshape(count * width, lanes))
        held_ref[step] = (mine + total_ref[:, span]).astype(out_ref.dtype)
        copies.append(pltpu.make_async_copy(held_ref.at[step], out_ref.at[:, span], sems.at[step]))
        copies[-1].start()
    for copy in copies:
        copy.wait()


def last_call(weights, first, blocks, total, dtype):
    rows, columns = total.shape
    steps = 4
    return pl.pallas_call(
        functools.partial(last_kernel, first),
        in_specs=[VMEM] * (2 + len(blocks)),
        out_specs=pl.BlockSpec(memory_space=pl.ANY),
        out_shape=jax.ShapeDtypeStruct((rows, columns), dtype),
        scratch_shapes=[
            pltpu.VMEM((steps, rows, columns // steps), dtype),
            pltpu.SemaphoreType.DMA((steps,)),
        ],
        compiler_params=pltpu.CompilerParams(vmem_limit_bytes=12 * 2**20),
        name="project_last",
    )(weights, *blocks, total)


VMEM = pl.BlockSpec(memory_space=pltpu.VMEM)


def cost(rows, depth, columns):
    return pl.CostEstimate(
        flops=2 * rows * depth * columns,
        bytes_accessed=2 * (rows + columns) * depth + 8 * rows * columns,
        transcendentals=0,
    )


def later_call(weights, first, blocks, total, dtype, name):
    rows, columns = total.shape
    depth = len(blocks) * weights.shape[1]
    return pl.pallas_call(
        functools.partial(later_kernel, first),
        in_specs=[VMEM] * (2 + len(blocks)),
        out_specs=VMEM,
        out_shape=jax.ShapeDtypeStruct((rows, columns), dtype),
        compiler_params=pltpu.CompilerParams(vmem_limit_bytes=12 * 2**20),
        cost_estimate=cost(rows, depth, columns),
        name=name,
    )(weights, *blocks, total)


def project(mixed, w_out):
    rows, width = mixed.shape
    columns = w_out.shape[1]
    weights = w_out.reshape(-1, width, columns)
    own = [(0, 0), (1, 0)]
    later = [(0, 1), (1, 1), (0, -1), (1, -1), (0, 2), (1, 2)]

    ahead = shifted(mixed, -1)
    beside = swapped(mixed)
    total, weights = pl.pallas_call(
        functools.partial(first_kernel, own, later),
        in_specs=[pl.BlockSpec(memory_space=pl.ANY), VMEM, VMEM],
        out_specs=[VMEM, VMEM],
        out_shape=[
            jax.ShapeDtypeStruct((rows, columns), jnp.float32),
            jax.ShapeDtypeStruct((len(later), width, columns), weights.dtype),
        ],
        scratch_shapes=[
            pltpu.VMEM((len(own), width, columns), weights.dtype),
            pltpu.SemaphoreType.DMA((len(own) + len(later),)),
        ],
        compiler_params=pltpu.CompilerParams(vmem_limit_bytes=44 * 2**20),
        cost_estimate=cost(rows, len(own) * width, columns),
        name="project_own",
    )(weights, mixed, beside)
    mixed, total = lax.optimization_barrier((mixed, total))
    behind = shifted(mixed, 1)
    ahead, total = lax.optimization_barrier((ahead, total))
    far = shifted(ahead, -1)
    total = later_call(weights, 0, [ahead, swapped(ahead)], total, jnp.float32, "project_middle")
    near_blocks = [behind, swapped(behind)]
    *near_blocks, far, total = lax.optimization_barrier((*near_blocks, far, total))
    beside_far = swapped(far)
    total = later_call(weights, 2, [*near_blocks, far], total, jnp.float32, "project_near")
    return last_call(weights, len(later) - 1, [beside_far], total, jnp.bfloat16)


def per_device(signal, gate, filt, skip, w_out):
    ways = lax.axis_size("ctx")
    rows, channels = signal.shape
    spread = lax.all_to_all(turn(signal, filt, ways), "ctx", 0, 0, tiled=True)
    conv = lax.all_to_all(convolve(spread), "ctx", 0, 0, tiled=True)
    return project(mix(conv.reshape(channels, rows), signal, gate, skip), w_out)


def solution(mesh):
    return jax.shard_map(
        per_device,
        mesh=mesh,
        in_specs=(P("ctx", "tp"), P("ctx", "tp"), P("ctx", "tp"), P("tp"), P(None, "tp")),
        out_specs=P("ctx", "tp"),
        check_vma=False,
    )
```

```python
import functools

import jax
import jax.numpy as jnp
import numpy as np
from jax import lax
from jax.experimental import pallas as pl
from jax.experimental.pallas import tpu as pltpu
from jax.sharding import PartitionSpec as P

GROUP = 16


def tables(blocks, rows):
    coarse, fine = 2 * blocks, rows // 2
    freq = np.arange(coarse) + 0.25
    turn = 2 * np.pi * np.outer(freq, np.arange(coarse)) / coarse
    turn = np.concatenate([turn[:, 0::2], turn[:, 1::2]], axis=1)
    same = np.eye(GROUP)
    outer = np.concatenate([np.kron(np.cos(turn), same), np.kron(-np.sin(turn), same)], axis=0)
    twist = np.repeat(2 * np.pi * np.outer(freq, np.arange(fine)) / (coarse * fine), GROUP, axis=0)
    index = np.arange(fine)
    inner = 2 * np.pi * (np.outer(index, index) % fine) / fine
    cos, sin = np.cos(inner), np.sin(inner)
    middle = np.block([[cos, -sin], [sin, cos]])
    return (
        np.concatenate([outer, middle], axis=0).astype(jnp.bfloat16),
        np.concatenate([np.cos(twist), np.sin(twist)], axis=1).astype(np.float32),
    )


def dot(left, right):
    return jnp.dot(left, right, preferred_element_type=jnp.float32)


def turn_kernel(signal_ref, filt_ref, out_ref):
    ways, share, _ = out_ref.shape
    rows = signal_ref.shape[0]
    for part, ref in enumerate((signal_ref, filt_ref)):
        flipped = ref[...].astype(jnp.float32).T.astype(jnp.bfloat16)
        out_ref[:, :, part * rows : (part + 1) * rows] = flipped.reshape(ways, share, rows)


def turn(signal, filt, ways):
    rows, channels = signal.shape
    return pl.pallas_call(
        turn_kernel,
        out_shape=jax.ShapeDtypeStruct((ways, channels // ways, 2 * rows), jnp.bfloat16),
        compiler_params=pltpu.CompilerParams(vmem_limit_bytes=12 * 2**20),
        name="turn",
    )(signal, filt)


def conv_kernel(x_ref, table_ref, twist_ref, out_ref):
    blocks, share, rows = out_ref.shape
    fine = rows // 2
    half = 2 * blocks * GROUP
    cos, sin = twist_ref[:, :fine], twist_ref[:, fine:]
    outer_ref, middle_ref = table_ref.at[: 2 * half], table_ref.at[2 * half :]
    scale = 1.0 / (blocks * rows)
    groups = [slice(start, start + GROUP) for start in range(0, share, GROUP)]

    def enter(group, lane):
        spans = [slice(lane, lane + fine), slice(lane + fine, lane + rows)]
        x = jnp.concatenate([x_ref[:, group, span].reshape(blocks * GROUP, fine) for span in spans], axis=0)
        return dot(outer_ref[...], x)

    def twist(a):
        re, im = a[:half], a[half:]
        return jnp.concatenate([re * cos + im * sin, im * cos - re * sin], axis=1).astype(jnp.bfloat16)

    def product(spec_x, spec_h):
        xr, xi, hr, hi = spec_x[:, :fine], spec_x[:, fine:], spec_h[:, :fine], spec_h[:, fine:]
        return jnp.concatenate([xr * hr - xi * hi, xr * hi + xi * hr], axis=1).astype(jnp.bfloat16)

    def back(prod):
        return lax.dot_general(
            prod, middle_ref[...], (((1,), (1,)), ((), ())), preferred_element_type=jnp.float32
        )

    def untwist(b):
        re, im = b[:, :fine], b[:, fine:]
        return jnp.concatenate([re * cos - im * sin, re * sin + im * cos], axis=0).astype(jnp.bfloat16)

    def leave(group, turned):
        y = scale * lax.dot_general(
            outer_ref[...], turned, (((0,), (0,)), ((), ())), preferred_element_type=jnp.float32
        )
        y = y.astype(jnp.bfloat16).reshape(2, blocks, GROUP, fine)
        out_ref[:, group, :fine] = y[0]
        out_ref[:, group, fine:] = y[1]

    entered = [[enter(group, lane) for lane in (0, rows)] for group in groups]
    spectra = dot(jnp.concatenate([twist(a) for pair in entered for a in pair], axis=0), middle_ref[...])
    spectra = [spectra[k * half : (k + 1) * half] for k in range(2 * len(groups))]
    returned = back(
        jnp.concatenate([product(*spectra[2 * k : 2 * k + 2]) for k in range(len(groups))], axis=0)
    )
    for k, group in enumerate(groups):
        leave(group, untwist(returned[k * half : (k + 1) * half]))


def convolve(x):
    blocks, share, rows = x.shape[0], x.shape[1], x.shape[2] // 2
    constants = [jnp.asarray(t) for t in tables(blocks, rows)]
    return pl.pallas_call(
        conv_kernel,
        out_shape=jax.ShapeDtypeStruct((blocks, share, rows), jnp.bfloat16),
        compiler_params=pltpu.CompilerParams(vmem_limit_bytes=20 * 2**20),
        name="convolve",
    )(x, *constants)


def mix_kernel(conv_ref, signal_ref, gate_ref, skip_ref, out_ref):
    conv = conv_ref[...].astype(jnp.float32).T
    values = signal_ref[...].astype(jnp.float32)
    out_ref[...] = (gate_ref[...].astype(jnp.float32) * (conv + skip_ref[...] * values)).astype(jnp.bfloat16)


def mix(conv, signal, gate, skip):
    rows, channels = signal.shape
    return pl.pallas_call(
        mix_kernel,
        out_shape=jax.ShapeDtypeStruct((rows, channels), jnp.bfloat16),
        compiler_params=pltpu.CompilerParams(vmem_limit_bytes=8 * 2**20),
        name="mix",
    )(conv, signal, gate, skip.reshape(1, channels))


def toward(device, step):
    count = lax.axis_size("tp")
    return (device + 2 * step * (1 - 2 * (device % 2)) + count) % count


def shifted(block, step):
    return lax.ppermute(block, "tp", [(i, toward(i, step)) for i in range(lax.axis_size("tp"))])


def swapped(block):
    return lax.ppermute(block, "tp", [(i, i ^ 1) for i in range(lax.axis_size("tp"))])


def rows_of(blocks):
    me = lax.axis_index("tp")
    return [toward(me ^ 1 if other else me, step) for other, step in blocks]


def first_kernel(own, later, weights_ref, mine_ref, beside_ref, total_ref, later_ref, held_ref, sems):
    copies = []
    for j, row in enumerate(rows_of(own)):
        copies.append(pltpu.make_async_copy(weights_ref.at[row], held_ref.at[j], sems.at[j]))
    for j, row in enumerate(rows_of(later)):
        copies.append(pltpu.make_async_copy(weights_ref.at[row], later_ref.at[j], sems.at[len(own) + j]))
    for copy in copies:
        copy.start()
    left = jnp.concatenate([mine_ref[...], beside_ref[...]], axis=1)
    for copy in copies[: len(own)]:
        copy.wait()
    add_product(left, held_ref, 0, None, total_ref)
    for copy in copies[len(own) :]:
        copy.wait()


def add_product(left, weights_ref, first, total_ref, out_ref):
    width = weights_ref.shape[1]
    count = left.shape[1] // width
    lanes = 256
    for start in range(0, out_ref.shape[1], lanes):
        span = slice(start, start + lanes)
        mine = dot(left, weights_ref[first : first + count, :, span].reshape(count * width, lanes))
        if total_ref is not None:
            mine = mine + total_ref[:, span]
        out_ref[:, span] = mine.astype(out_ref.dtype)


def later_kernel(first, weights_ref, *refs):
    blocks, total_ref, out_ref = refs[:-2], refs[-2], refs[-1]
    left = jnp.concatenate([block[...] for block in blocks], axis=1)
    add_product(left, weights_ref, first, total_ref, out_ref)


def last_kernel(first, weights_ref, *refs):
    blocks, total_ref, out_ref, held_ref, sems = refs[:-4], refs[-4], refs[-3], refs[-2], refs[-1]
    left = jnp.concatenate([block[...] for block in blocks], axis=1)
    count, width = len(blocks), weights_ref.shape[1]
    right = weights_ref[first : first + count].reshape(count * width, weights_ref.shape[2])
    high = held_ref.shape[1]
    copies = []
    for step in range(held_ref.shape[0]):
        span = slice(step * high, (step + 1) * high)
        held_ref[step] = (dot(left[span], right) + total_ref[span, :]).astype(out_ref.dtype)
        copies.append(pltpu.make_async_copy(held_ref.at[step], out_ref.at[pl.ds(step * high, high)], sems.at[step]))
        copies[-1].start()
    for copy in copies:
        copy.wait()


def last_call(weights, first, blocks, total, dtype):
    rows, columns = total.shape
    steps = 4
    return pl.pallas_call(
        functools.partial(last_kernel, first),
        in_specs=[VMEM] * (2 + len(blocks)),
        out_specs=pl.BlockSpec(memory_space=pl.ANY),
        out_shape=jax.ShapeDtypeStruct((rows, columns), dtype),
        scratch_shapes=[
            pltpu.VMEM((steps, rows // steps, columns), dtype),
            pltpu.SemaphoreType.DMA((steps,)),
        ],
        compiler_params=pltpu.CompilerParams(vmem_limit_bytes=12 * 2**20),
        name="project_last",
    )(weights, *blocks, total)


VMEM = pl.BlockSpec(memory_space=pltpu.VMEM)


def cost(rows, depth, columns):
    return pl.CostEstimate(
        flops=2 * rows * depth * columns,
        bytes_accessed=2 * (rows + columns) * depth + 8 * rows * columns,
        transcendentals=0,
    )


def later_call(weights, first, blocks, total, dtype, name):
    rows, columns = total.shape
    depth = len(blocks) * weights.shape[1]
    return pl.pallas_call(
        functools.partial(later_kernel, first),
        in_specs=[VMEM] * (2 + len(blocks)),
        out_specs=VMEM,
        out_shape=jax.ShapeDtypeStruct((rows, columns), dtype),
        compiler_params=pltpu.CompilerParams(vmem_limit_bytes=12 * 2**20),
        cost_estimate=cost(rows, depth, columns),
        name=name,
    )(weights, *blocks, total)


def project(mixed, w_out):
    rows, width = mixed.shape
    columns = w_out.shape[1]
    weights = w_out.reshape(-1, width, columns)
    own = [(0, 0), (1, 0)]
    later = [(0, 1), (1, 1), (0, -1), (1, -1), (0, 2), (1, 2)]

    ahead = shifted(mixed, -1)
    beside = swapped(mixed)
    total, weights = pl.pallas_call(
        functools.partial(first_kernel, own, later),
        in_specs=[pl.BlockSpec(memory_space=pl.ANY), VMEM, VMEM],
        out_specs=[VMEM, VMEM],
        out_shape=[
            jax.ShapeDtypeStruct((rows, columns), jnp.float32),
            jax.ShapeDtypeStruct((len(later), width, columns), weights.dtype),
        ],
        scratch_shapes=[
            pltpu.VMEM((len(own), width, columns), weights.dtype),
            pltpu.SemaphoreType.DMA((len(own) + len(later),)),
        ],
        compiler_params=pltpu.CompilerParams(vmem_limit_bytes=44 * 2**20),
        cost_estimate=cost(rows, len(own) * width, columns),
        name="project_own",
    )(weights, mixed, beside)
    mixed, total = lax.optimization_barrier((mixed, total))
    behind = shifted(mixed, 1)
    ahead, total = lax.optimization_barrier((ahead, total))
    far = shifted(ahead, -1)
    total = later_call(weights, 0, [ahead, swapped(ahead), behind], total, jnp.float32, "project_middle")
    near_blocks = [swapped(behind)]
    *near_blocks, far, total = lax.optimization_barrier((*near_blocks, far, total))
    beside_far = swapped(far)
    total = later_call(weights, 3, [*near_blocks, far], total, jnp.float32, "project_near")
    return last_call(weights, len(later) - 1, [beside_far], total, jnp.bfloat16)


def per_device(signal, gate, filt, skip, w_out):
    ways = lax.axis_size("ctx")
    rows, channels = signal.shape
    spread = lax.all_to_all(turn(signal, filt, ways), "ctx", 0, 0, tiled=True)
    conv = lax.all_to_all(convolve(spread), "ctx", 0, 0, tiled=True)
    return project(mix(conv.reshape(channels, rows), signal, gate, skip), w_out)


def solution(mesh):
    return jax.shard_map(
        per_device,
        mesh=mesh,
        in_specs=(P("ctx", "tp"), P("ctx", "tp"), P("ctx", "tp"), P("tp"), P(None, "tp")),
        out_specs=P("ctx", "tp"),
        check_vma=False,
    )
```
